512 devices in a mesh: inp: 4 (over y), out: 8 (over z_hi, core), dep: 16 (over z_lo, x).
Axes of the slice: x: 4, y: 4, z: 16 (z_hi: 4, z_lo: 4; z = z_hi * 4 + z_lo), core: 2. Of those that a mesh axis runs over, the one named last changes fastest.
Arguments:
- x_saved: bfloat16 [1024, 8192], P('dep', ('inp', 'out')), may hold values from -6 to 6
- gate_pre: bfloat16 [1024, 14336], P(('inp', 'out'), 'dep'), may hold values from -6 to 6
- up_pre: bfloat16 [1024, 14336], P(('inp', 'out'), 'dep'), may hold values from -6 to 6
- out_grad: bfloat16 [1024, 8192], P('dep', ('inp', 'out')), may hold values from -6 to 6
- gate_weight: bfloat16 [8192, 14336], P(('inp', 'out'), 'dep'), may hold values from -0.09375 to 0.09375
- up_weight: bfloat16 [8192, 14336], P(('inp', 'out'), 'dep'), may hold values from -0.09375 to 0.09375
- down_weight: bfloat16 [14336, 8192], P('dep', ('inp', 'out')), may hold values from -0.0625 to 0.0625
- gate_mask: int32 [64, 112], P(('inp', 'out'), 'dep'), may hold values 0 or 1
- up_mask: int32 [64, 112], P(('inp', 'out'), 'dep'), may hold values 0 or 1
- down_mask: int32 [112, 64], P('dep', ('inp', 'out')), may hold values 0 or 1
Outputs:
- input_grad: bfloat16 [1024, 8192], P('dep', ('inp', 'out'))
- gate_weight_grad: float32 [8192, 14336], P(('inp', 'out'), 'dep')
- up_weight_grad: float32 [8192, 14336], P(('inp', 'out'), 'dep')
- down_weight_grad: float32 [14336, 8192], P('dep', ('inp', 'out'))
The draws below stay inside these ranges and needn't reach their ends.
Inputs may be any that keep to these rules, and one draw needn't show every extreme that they name: `gate_mask`: 1 keeps a 128 x 128 tile of the gate projection, 0 drops it. `up_mask`: 1 keeps a 128 x 128 tile of the up projection, 0 drops it. `down_mask`: 1 keeps a 128 x 128 tile of the down projection, 0 drops it.
All inputs are finite; a program needn't handle non-finite values. No bound on the sum of `gate_mask` or of `up_mask` or of `down_mask` on one device may be relied on, other than what follows from the above.
Results may differ from the reference program's by a relative error of at most 0.0049.
Values may be sent and summed in bfloat16 or wider, within the bound.
A program may use at most 64 MiB of HBM per device.

```python
import jax
import jax.numpy as jnp

D = 8192
FF = 14336
TILE = 128
TOKENS = 1024


def plant(values, stream_key, smallest, top_value):
    longest = values.shape.index(max(values.shape))
    spots = []
    for shift in (0, 1):
        where = [jax.random.randint(jax.random.fold_in(stream_key, axis), (), 0, length) for axis, length in enumerate(values.shape)]
        where[longest] = (where[longest] + shift) % values.shape[longest]
        spots.append(tuple(where))
    return values.at[spots[0]].set(smallest).at[spots[1]].set(top_value)


def block_scale(rng, extent, pieces, least, largest):
    def one(axis_at, parts):
        steps = jax.random.uniform(jax.random.fold_in(jax.random.fold_in(rng, 6), axis_at), (parts,), jnp.float32, least / len(pieces), largest / len(pieces))
        return jnp.repeat(jnp.exp(steps), extent[axis_at] // parts).reshape((-1,) + (1,) * (len(extent) - axis_at - 1))

    gain = one(*pieces[0])
    for cut in pieces[1:]:
        gain = gain * one(*cut)
    return gain


def normal_values(rng, shape, deviation, bound, split=(), kind=jnp.bfloat16):
    values = deviation * jax.random.normal(rng, shape, jnp.float32)
    if split:
        values = values * block_scale(rng, shape, split, -0.22, 0.18)
    return jnp.clip(values, -bound, bound).astype(kind)


def setup_inputs(seed: int = 0) -> dict:
    splits = jax.random.split(jax.random.key(seed), 11)
    x_saved = normal_values(splits[0], (TOKENS, D), 1.0, 6.0, ((0, 16), (1, 32)))
    gate_pre = normal_values(splits[1], (TOKENS, FF), 1.5, 6.0, ((0, 32), (1, 16)))
    up_pre = normal_values(splits[2], (TOKENS, FF), 1.0, 6.0, ((0, 32), (1, 16)))
    out_grad = normal_values(splits[3], (TOKENS, D), 1.0, 6.0, ((0, 16), (1, 32)))
    gate_weight = normal_values(splits[4], (D, FF), (D // 2) ** -0.5, 0.09375, ((0, 32), (1, 16)))
    up_weight = normal_values(splits[5], (D, FF), (D // 2) ** -0.5, 0.09375, ((0, 32), (1, 16)))
    down_weight = normal_values(splits[6], (FF, D), (FF // 2) ** -0.5, 0.0625, ((0, 16), (1, 32)))
    gate_mask = plant((jax.random.randint(splits[7], (D // TILE, FF // TILE), 0, 2) < 1).astype(jnp.int32), jax.random.fold_in(splits[7], 1), 0, 1)
    up_mask = plant((jax.random.randint(splits[8], (D // TILE, FF // TILE), 0, 2) < 1).astype(jnp.int32), jax.random.fold_in(splits[8], 1), 0, 1)
    down_mask = plant((jax.random.randint(splits[9], (FF // TILE, D // TILE), 0, 2) < 1).astype(jnp.int32), jax.random.fold_in(splits[9], 1), 0, 1)
    return {"x_saved": x_saved, "gate_pre": gate_pre, "up_pre": up_pre, "out_grad": out_grad, "gate_weight": gate_weight, "up_weight": up_weight, "down_weight": down_weight, "gate_mask": gate_mask, "up_mask": up_mask, "down_mask": down_mask}


def expand(tiles):
    return jnp.repeat(jnp.repeat(tiles, TILE, 0), TILE, 1).astype(jnp.bfloat16)


def reference(x_saved, gate_pre, up_pre, out_grad, gate_weight, up_weight, down_weight, gate_mask, up_mask, down_mask):
    gate_keep = expand(gate_mask)
    up_keep = expand(up_mask)
    down_keep = expand(down_mask)
    gate_eff = gate_weight * gate_keep
    up_eff = up_weight * up_keep
    down_eff = down_weight * down_keep
    hidden_grad = jnp.dot(out_grad, down_eff.T, preferred_element_type=jnp.float32)
    gate_val = gate_pre.astype(jnp.float32)
    up_val = up_pre.astype(jnp.float32)
    sigma = jax.nn.sigmoid(gate_val)
    gate_grad = (hidden_grad * up_val * sigma * (1.0 + gate_val * (1.0 - sigma))).astype(jnp.bfloat16)
    up_grad = (hidden_grad * gate_val * sigma).astype(jnp.bfloat16)
    hidden_act = (gate_val * sigma * up_val).astype(jnp.bfloat16)
    down_weight_grad = jnp.dot(hidden_act.T, out_grad, preferred_element_type=jnp.float32) * down_keep.astype(jnp.float32)
    gate_weight_grad = jnp.dot(x_saved.T, gate_grad, preferred_element_type=jnp.float32) * gate_keep.astype(jnp.float32)
    up_weight_grad = jnp.dot(x_saved.T, up_grad, preferred_element_type=jnp.float32) * up_keep.astype(jnp.float32)
    input_grad = (jnp.dot(gate_grad, gate_eff.T, preferred_element_type=jnp.float32)
                  + jnp.dot(up_grad, up_eff.T, preferred_element_type=jnp.float32)).astype(jnp.bfloat16)
    return input_grad, gate_weight_grad, up_weight_grad, down_weight_grad
```

```python
import functools

import jax
import jax.numpy as jnp
from jax import lax
from jax.experimental import pallas as pl
from jax.experimental.pallas import tpu as pltpu
from jax.sharding import PartitionSpec as P

TILE = 128
MESH = pl.DeviceIdType.MESH
F32 = jnp.float32
BF16 = jnp.bfloat16
NT = (((1,), (1,)), ((), ()))
TN = (((0,), (0,)), ((), ()))


def dot(left, right, dims):
    return lax.dot_general(left, right, dims, preferred_element_type=F32)


class Sems:
    def __init__(self, send, recv):
        self.send, self.recv = send, recv
        self.sends = self.recvs = 0
        self.started = []

    def take(self, count=1):
        first = self.recvs
        self.recvs += count
        return first

    def start(self, src, dst, slot, device):
        copy = pltpu.make_async_remote_copy(
            src_ref=src,
            dst_ref=dst,
            send_sem=self.send.at[self.sends],
            recv_sem=self.recv.at[slot],
            device_id=device,
            device_id_type=MESH,
        )
        self.sends += 1
        copy.start()
        self.started.append(copy)

    def wait(self, dst, slot, device):
        pltpu.make_async_remote_copy(
            src_ref=dst,
            dst_ref=dst,
            send_sem=self.send.at[0],
            recv_sem=self.recv.at[slot],
            device_id=device,
            device_id_type=MESH,
        ).wait_recv()

    def drain(self):
        for copy in self.started:
            copy.wait_send()


def keep_tiles(ref, mask, where=()):
    rows, cols = mask.shape
    for i in range(rows):
        for j in range(cols):
            at = (*where, pl.ds(i * TILE, TILE), pl.ds(j * TILE, TILE))
            ref[at] = (ref[at].astype(F32) * mask[i, j].astype(F32)).astype(ref.dtype)


def kernel(
    x_in, g_in, u_in, og_in, gw_in, uw_in, dw_in, gm, um, dm,
    ig_out, gwg_out, uwg_out, dwg_out,
    cot, cot_other, xs, act, gu, g_val, u_val, gw, uw, dw, f_gate, f_up,
    part_own, part_send, part_recv, sum_send, sum_recv,
    ig_own, ig_send, ig_recv, ig_mine, zl_send, zl_recv, ig_res,
    gwg, uwg, dwg, local, send, recv, zl_ss, zl_rs,
):
    y = lax.axis_index("inp")
    out = lax.axis_index("out")
    dep = lax.axis_index("dep")
    zh, c = out // 2, out % 2
    zl, x = dep // 4, dep % 4
    other = 1 - c
    plus = lambda v, k: (v + k) % 4
    at_core = {"out": zh * 2 + other}
    at_y = lambda k: {"inp": plus(y, k)}
    at_zh = lambda k: {"out": plus(zh, k) * 2 + c}
    at_x = lambda k: {"dep": zl * 4 + plus(x, k)}
    at_zl = lambda k, core: {"out": zh * 2 + core, "dep": plus(zl, k) * 4 + x}

    loads = []

    def load(src, dst):
        copy = pltpu.make_async_copy(src, dst, local.at[len(loads)])
        copy.start()
        loads.append(copy)
        return copy

    ld_og = load(og_in.at[pl.ds(c, 1)], cot.at[c, zl, pl.ds(x, 1)])
    ld_g = load(g_in, g_val)
    ld_u = load(u_in, u_val)
    ld_dw = load(dw_in, dw.at[c])
    ld_x = load(x_in, xs.at[:, zl, x])
    ld_gw = load(gw_in, gw)
    ld_uw = load(uw_in, uw)

    peers = [at_core]
    for k in (1, 2, 3):
        peers += [at_y(k), at_zh(k), at_x(k), at_zl(k, 0), at_zl(k, 1)]
    barrier = pltpu.get_barrier_semaphore()
    for device in peers:
        pl.semaphore_signal(barrier, inc=1, device_id=device, device_id_type=MESH)
    pl.semaphore_wait(barrier, len(peers))

    sems = Sems(send, recv)

    og_slot = sems.take(8)
    sems.start(og_in.at[other], cot.at[c, zl, x], og_slot + c, at_core)
    for k in (2, 1, 3):
        for h in (0, 1):
            sems.start(og_in.at[h], cot.at[c, zl, x], og_slot + 2 * k + c, at_zl(k, h))

    ld_g.wait()
    ld_u.wait()
    g = g_val[...].astype(F32)
    u = u_val[...].astype(F32)
    s = 1.0 / (1.0 + jnp.exp(-g))
    gs = g * s
    act[c, y, zh] = (gs * u).astype(BF16)
    f_up[...] = gs
    f_gate[...] = u * s * (1.0 + g * (1.0 - s))

    act_z = sems.take(4)
    act_y = sems.take(16)
    for k in (2, 1, 3):
        sems.start(act.at[c, y, zh], act.at[c, y, zh], act_z + k, at_zh(k))

    def act_to_y(kz):
        block = act.at[c, y, plus(zh, -kz)]
        for k in (2, 1, 3):
            sems.start(block, block, act_y + 4 * k + kz, at_y(k))

    act_to_y(0)

    ld_dw.wait()
    keep_tiles(dw, dm, (c,))
    dw_slot = sems.take()
    sems.start(dw.at[c], dw.at[c], dw_slot, at_core)

    ld_og.wait()
    sems.wait(cot.at[other, zl, x], og_slot + other, at_core)
    for k in (1, 3, 2):
        for f in (0, 1):
            sems.wait(cot.at[f, plus(zl, -k), x], og_slot + 2 * k + f, at_core)
    og_x = sems.take(4)
    for k in (2, 1, 3):
        sems.start(cot.at[:, :, x], cot.at[:, :, x], og_x + k, at_x(k))

    x_zl = sems.take(4)
    for k in (2, 1, 3):
        sems.start(x_in, xs.at[:, zl, x], x_zl + k, at_zl(k, c))

    ld_gw.wait()
    keep_tiles(gw, gm)
    ld_uw.wait()
    keep_tiles(uw, um)
    sems.wait(dw.at[other], dw_slot, at_core)
    for k in (1, 3):
        sems.wait(act.at[c, y, plus(zh, -k)], act_z + k, at_core)
        act_to_y(k)

    for k in (1, 3, 2):
        sems.wait(cot.at[:, :, plus(x, -k)], og_x + k, at_core)

    def partial(group):
        rows = [cot[f, group].reshape(128, 256) for f in (0, 1)]
        return dot(rows[0], dw[0], NT) + dot(rows[1], dw[1], NT)

    for k in (2, 1, 3):
        part_send[k - 1] = partial(plus(y, k)).astype(BF16).reshape(4, 32, 896)
    part_y = sems.take(16)
    for kz in (2, 1, 3, 0):
        block = plus(zh, kz)
        for k in (2, 1, 3):
            sems.start(
                part_send.at[k - 1, block], part_recv.at[k - 1, kz], part_y + 4 * k + kz, at_y(k)
            )
    part_own[...] = partial(y).reshape(4, 32, 896)

    cot_slot = sems.take()
    sems.start(cot.at[other], cot_other, cot_slot, at_core)

    ld_x.wait()
    for k in (1, 3, 2):
        sems.wait(xs.at[:, plus(zl, -k), x], x_zl + k, at_core)
    x_x = sems.take(4)
    for k in (2, 1, 3):
        sems.start(xs.at[:, :, x], xs.at[:, :, x], x_x + k, at_x(k))

    sems.wait(act.at[c, y, plus(zh, -2)], act_z + 2, at_core)
    act_to_y(2)

    sum_z = sems.take(4)
    total = None
    for kz in (2, 1, 3, 0):
        for k in (1, 3, 2):
            sems.wait(part_recv.at[k - 1, kz], part_y + 4 * k + kz, at_core)
        total = part_own[plus(zh, kz)]
        for k in (1, 2, 3):
            total = total + part_recv[k - 1, kz].astype(F32)
        if kz:
            sum_send[kz - 1] = total.astype(BF16)
            sems.start(sum_send.at[kz - 1], sum_recv.at[kz - 1], sum_z + kz, at_zh(kz))
    for kz in (1, 3, 2):
        sems.wait(sum_recv.at[kz - 1], sum_z + kz, at_core)
        total = total + sum_recv[kz - 1].astype(F32)

    gu[0, c, y, zh] = (total * f_gate[...]).astype(BF16)
    gu[1, c, y, zh] = (total * f_up[...]).astype(BF16)
    gu_z = sems.take(4)
    gu_y = sems.take(16)
    gu_c = sems.take(4)
    for k in (2, 1, 3):
        block = gu.at[:, c, y, zh]
        sems.start(block, block, gu_z + k, at_zh(k))

    def gu_to_y(kz):
        block = gu.at[:, c, y, plus(zh, -kz)]
        for k in (2, 1, 3):
            sems.start(block, block, gu_y + 4 * k + kz, at_y(k))

    gu_to_y(0)

    for k in (1, 3, 2):
        for kz in range(4):
            sems.wait(act.at[c, plus(y, -k), plus(zh, -kz)], act_y + 4 * k + kz, at_core)
    act_c = sems.take()
    sems.start(act.at[c], act.at[c], act_c, at_core)
    sems.wait(cot_other, cot_slot, at_core)
    sems.wait(act.at[other], act_c, at_core)
    mine = cot[c].reshape(512, 256)
    theirs = cot_other[...].reshape(512, 256)
    for i in range(7):
        at = pl.ds(i * TILE, TILE)
        tile = dot(act[c, :, :, :, at].reshape(512, TILE), mine, TN)
        tile = tile + dot(act[other, :, :, :, at].reshape(512, TILE), theirs, TN)
        for j in range(2):
            dwg[at, pl.ds(j * TILE, TILE)] = (
                tile[:, j * TILE : (j + 1) * TILE] * dm[i, j].astype(F32)
            )
    stores = [load(dwg, dwg_out)]

    for k in (1, 3, 2):
        sems.wait(xs.at[:, :, plus(x, -k)], x_x + k, at_core)

    for k in (1, 3, 2):
        sems.wait(gu.at[:, c, y, plus(zh, -k)], gu_z + k, at_core)
        gu_to_y(k)

    ig_x = sems.take(16)
    order = (0, 1, 3, 2)

    def reduce_x(k):
        group = plus(y, -k)
        for j in (1, 3, 2):
            sems.wait(ig_recv.at[k, j - 1], ig_x + 4 * k + j, at_core)
        value = ig_own[k]
        for j in (0, 1, 2):
            value = value + ig_recv[k, j].astype(F32)

        @pl.when(group == zl)
        def _():
            ig_mine[...] = value

        @pl.when(group != zl)
        def _():
            zl_send[k] = value.astype(BF16)
            to_zl(k).start()

    def to_zl(k):
        group = plus(y, -k)
        return pltpu.make_async_remote_copy(
            src_ref=zl_send.at[k],
            dst_ref=zl_recv.at[zl],
            send_sem=zl_ss.at[k],
            recv_sem=zl_rs.at[zl],
            device_id={"dep": group * 4 + x},
            device_id_type=MESH,
        )

    for n, k in enumerate(order):
        group = plus(y, -k)
        if k:
            for kz in (0, 1, 3, 2):
                sems.wait(gu.at[:, c, group, plus(zh, -kz)], gu_y + 4 * k + kz, at_core)
        sems.start(gu.at[:, c, group], gu.at[:, c, group], gu_c + k, at_core)
        sems.wait(gu.at[:, other, group], gu_c + k, at_core)
        gate = gu[0, :, group].reshape(256, 896)
        up = gu[1, :, group].reshape(256, 896)
        rows = (dot(gate, gw[...], NT) + dot(up, uw[...], NT)).reshape(2, 4, 32, 256)
        ig_send[k] = rows.astype(BF16)
        for j in (2, 1, 3):
            sems.start(
                ig_send.at[k, :, plus(x, j)], ig_recv.at[k, j - 1], ig_x + 4 * k + j, at_x(j)
            )
        ig_all = rows
        mine_rows = jnp.zeros((2, 32, 256), F32)
        for j in range(4):
            mine_rows = jnp.where(x == j, ig_all[:, j], mine_rows)
        ig_own[k] = mine_rows
        if n:
            reduce_x(order[n - 1])
        left = xs[:, group].reshape(256, 256)
        for total_ref, rows_in in ((gwg, gate), (uwg, up)):
            product = dot(left, rows_in, TN)
            if n:
                product = product + total_ref[...]
            total_ref[...] = product
    keep_tiles(gwg, gm)
    stores.append(load(gwg, gwg_out))
    keep_tiles(uwg, um)
    stores.append(load(uwg, uwg_out))
    reduce_x(order[-1])

    value = ig_mine[...]
    for k in (1, 2, 3):
        sems_at = plus(zl, k)
        pltpu.make_async_remote_copy(
            src_ref=zl_recv.at[sems_at],
            dst_ref=zl_recv.at[sems_at],
            send_sem=zl_ss.at[0],
            recv_sem=zl_rs.at[sems_at],
            device_id=at_core,
            device_id_type=MESH,
        ).wait_recv()
        value = value + zl_recv[sems_at].astype(F32)
    ig_res[...] = value.astype(BF16)
    stores.append(load(ig_res, ig_out))
    sems.drain()
    for k in range(4):

        @pl.when(plus(y, -k) != zl)
        def _():
            to_zl(k).wait_send()

    for copy in stores:
        copy.wait()


SENDS = 128
RECVS = 128


def on_device(x_saved, gate_pre, up_pre, out_grad, gate_weight, up_weight, down_weight, gate_mask, up_mask, down_mask):
    any_ = pl.BlockSpec(memory_space=pl.ANY)
    smem = pl.BlockSpec(memory_space=pltpu.SMEM)
    vmem = lambda *shape: pltpu.VMEM(shape, BF16)
    vmem32 = lambda *shape: pltpu.VMEM(shape, F32)
    outs = pl.pallas_call(
        kernel,
        name="backward",
        out_shape=(
            jax.ShapeDtypeStruct((2, 32, 256), BF16),
            jax.ShapeDtypeStruct((256, 896), F32),
            jax.ShapeDtypeStruct((256, 896), F32),
            jax.ShapeDtypeStruct((896, 256), F32),
        ),
        in_specs=[any_] * 7 + [smem] * 3,
        out_specs=(any_,) * 4,
        scratch_shapes=[
            vmem(2, 4, 4, 32, 256),
            vmem(4, 4, 32, 256),
            vmem(2, 4, 4, 32, 256),
            vmem(2, 4, 4, 32, 896),
            vmem(2, 2, 4, 4, 32, 896),
            vmem(32, 896),
            vmem(32, 896),
            vmem(256, 896),
            vmem(256, 896),
            vmem(2, 896, 256),
            vmem32(32, 896),
            vmem32(32, 896),
            vmem32(4, 32, 896),
            vmem(3, 4, 32, 896),
            vmem(3, 4, 32, 896),
            vmem(3, 32, 896),
            vmem(3, 32, 896),
            vmem32(4, 2, 32, 256),
            vmem(4, 2, 4, 32, 256),
            vmem(4, 3, 2, 32, 256),
            vmem32(2, 32, 256),
            vmem(4, 2, 32, 256),
            vmem(4, 2, 32, 256),
            vmem(2, 32, 256),
            vmem32(256, 896),
            vmem32(256, 896),
            vmem32(896, 256),
            pltpu.SemaphoreType.DMA((16,)),
            pltpu.SemaphoreType.DMA((SENDS,)),
            pltpu.SemaphoreType.DMA((RECVS,)),
            pltpu.SemaphoreType.DMA((4,)),
            pltpu.SemaphoreType.DMA((4,)),
        ],
        compiler_params=pltpu.CompilerParams(
            collective_id=0, has_side_effects=True, vmem_limit_bytes=48 << 20
        ),
    )(
        x_saved.reshape(2, 32, 256), gate_pre, up_pre, out_grad.reshape(2, 32, 256),
        gate_weight, up_weight, down_weight, gate_mask, up_mask, down_mask,
    )
    return (outs[0].reshape(64, 256), *outs[1:])


def solution(mesh):
    return jax.shard_map(
        on_device,
        mesh=mesh,
        in_specs=(
            P("dep", ("inp", "out")),
            P(("inp", "out"), "dep"),
            P(("inp", "out"), "dep"),
            P("dep", ("inp", "out")),
            P(("inp", "out"), "dep"),
            P(("inp", "out"), "dep"),
            P("dep", ("inp", "out")),
            P(("inp", "out"), "dep"),
            P(("inp", "out"), "dep"),
            P("dep", ("inp", "out")),
        ),
        out_specs=(
            P("dep", ("inp", "out")),
            P(("inp", "out"), "dep"),
            P(("inp", "out"), "dep"),
            P("dep", ("inp", "out")),
        ),
        check_vma=False,
    )
```

```python
import functools

import jax
import jax.numpy as jnp
from jax import lax
from jax.experimental import pallas as pl
from jax.experimental.pallas import tpu as pltpu
from jax.sharding import PartitionSpec as P

TILE = 128
MESH = pl.DeviceIdType.MESH
F32 = jnp.float32
BF16 = jnp.bfloat16
NT = (((1,), (1,)), ((), ()))
TN = (((0,), (0,)), ((), ()))


def dot(left, right, dims):
    return lax.dot_general(left, right, dims, preferred_element_type=F32)


class Sems:
    def __init__(self, send, recv):
        self.send, self.recv = send, recv
        self.sends = self.recvs = 0
        self.started = []

    def take(self, count=1):
        first = self.recvs
        self.recvs += count
        return first

    def start(self, src, dst, slot, device):
        copy = pltpu.make_async_remote_copy(
            src_ref=src,
            dst_ref=dst,
            send_sem=self.send.at[self.sends],
            recv_sem=self.recv.at[slot],
            device_id=device,
            device_id_type=MESH,
        )
        self.sends += 1
        copy.start()
        self.started.append(copy)
        return copy

    def settle(self, copies):
        for copy in copies:
            copy.wait_send()
            self.started = [one for one in self.started if one is not copy]

    def wait(self, dst, slot, device):
        pltpu.make_async_remote_copy(
            src_ref=dst,
            dst_ref=dst,
            send_sem=self.send.at[0],
            recv_sem=self.recv.at[slot],
            device_id=device,
            device_id_type=MESH,
        ).wait_recv()

    def drain(self):
        for copy in self.started:
            copy.wait_send()


def keep_tiles(ref, mask, tiles=(2, 7), where=()):
    rows, cols = tiles
    for i in range(rows):
        for j in range(cols):
            at = (*where, pl.ds(i * TILE, TILE), pl.ds(j * TILE, TILE))
            ref[at] = (ref[at].astype(F32) * mask(i, j).astype(F32)).astype(ref.dtype)


def kernel(
    x_in, g_in, u_in, og_in, gw_in, uw_in, dw_in, gm_in, um_in, dm_in,
    ig_out, gwg_out, uwg_out, dwg_out,
    cot, cot_other, xs, pre, hid, f_gate, f_up, act, gate, up, gw, uw, dw,
    part_own, part_send, part_recv, sum_send, sum_recv,
    ig_own, ig_send, ig_recv, ig_mine, zl_send, zl_recv, ig_res,
    gwg, uwg, dwg, gm, um, dm, local, send, recv, zl_ss, zl_rs,
):
    y = lax.axis_index("inp")
    out = lax.axis_index("out")
    dep = lax.axis_index("dep")
    zh, c = out // 2, out % 2
    zl, x = dep // 4, dep % 4
    other = 1 - c
    plus = lambda v, k: (v + k) % 4
    at_core = {"out": zh * 2 + other}
    at_y = lambda k: {"inp": plus(y, k)}
    at_zh = lambda k: {"out": plus(zh, k) * 2 + c}
    at_x = lambda k: {"dep": zl * 4 + plus(x, k)}
    at_zl = lambda k, core: {"out": zh * 2 + core, "dep": plus(zl, k) * 4 + x}

    loads = []

    def load(src, dst):
        copy = pltpu.make_async_copy(src, dst, local.at[len(loads)])
        copy.start()
        loads.append(copy)
        return copy


    def wait_load(copy):
        copy.wait()

    ld_og = load(og_in.at[pl.ds(c, 1)], cot.at[c, zl, pl.ds(x, 1)])
    ld_g = load(g_in, pre.at[0, c, y, zh])
    ld_u = load(u_in, pre.at[1, c, y, zh])
    ld_dw = load(dw_in, dw.at[c])
    ld_masks = [load(dm_in, dm), load(gm_in, gm), load(um_in, um)]
    ld_x = load(x_in, xs.at[:, zl, x])
    ld_gw = load(gw_in, gw)
    ld_uw = load(uw_in, uw)

    peers = [at_core]
    for k in (1, 2, 3):
        peers += [at_y(k), at_zh(k), at_x(k), at_zl(k, 0), at_zl(k, 1)]
    barrier = pltpu.get_barrier_semaphore()
    for device in peers:
        pl.semaphore_signal(barrier, inc=1, device_id=device, device_id_type=MESH)
    pl.semaphore_wait(barrier, len(peers))

    sems = Sems(send, recv)

    og_slot = sems.take(8)
    sems.start(og_in.at[other], cot.at[c, zl, x], og_slot + c, at_core)
    for k in (2, 1, 3):
        for h in (0, 1):
            sems.start(og_in.at[h], cot.at[c, zl, x], og_slot + 2 * k + c, at_zl(k, h))

    pre_z = sems.take(4)
    pre_y = sems.take(16)
    pre_c = sems.take(4)

    def pre_to_y(kz):
        block = pre.at[:, c, y, plus(zh, -kz)]
        return [sems.start(block, block, pre_y + 4 * k + kz, at_y(k)) for k in (1, 3, 2)]

    wait_load(ld_g)
    wait_load(ld_u)
    pre_to_y(0)

    def pre_to_z(k):
        block = pre.at[:, c, y, zh]
        sems.start(block, block, pre_z + k, at_zh(k))


    wait_load(ld_dw)
    for copy in ld_masks:
        wait_load(copy)
    keep_tiles(dw, lambda i, j: dm[j, i], (7, 2), (c,))
    dw_slot = sems.take()
    sems.start(dw.at[c], dw.at[c], dw_slot, at_core)

    wait_load(ld_og)
    sems.wait(cot.at[other, zl, x], og_slot + other, at_core)
    for k in (1, 3, 2):
        for f in (0, 1):
            sems.wait(cot.at[f, plus(zl, -k), x], og_slot + 2 * k + f, at_core)
    og_x = sems.take(4)
    for k in (2, 1, 3):
        sems.start(cot.at[:, :, x], cot.at[:, :, x], og_x + k, at_x(k))
    pre_to_z(1)
    pre_to_z(3)

    x_zl = sems.take(4)
    x_x = sems.take(4)
    for k in (2, 1, 3):
        sems.start(x_in, xs.at[:, zl, x], x_zl + k, at_zl(k, c))

    wait_load(ld_gw)
    keep_tiles(gw, lambda i, j: gm[i, j])
    wait_load(ld_uw)
    keep_tiles(uw, lambda i, j: um[i, j])
    sems.wait(dw.at[other], dw_slot, at_core)
    for k in (1, 3, 2):
        sems.wait(cot.at[:, :, plus(x, -k)], og_x + k, at_core)

    def partial(group):
        rows = [cot[f, group].reshape(128, 256) for f in (0, 1)]
        return dot(rows[0], dw[0], NT) + dot(rows[1], dw[1], NT)

    for k in (2, 1, 3):
        part_send[k - 1] = partial(plus(y, k)).astype(BF16).reshape(4, 32, 896)
    part_y = sems.take(16)
    for kz in (2, 1, 3, 0):
        block = plus(zh, kz)
        for k in (2, 1, 3):
            sems.start(
                part_send.at[k - 1, block], part_recv.at[k - 1, kz], part_y + 4 * k + kz, at_y(k)
            )
    part_own[...] = partial(y).reshape(4, 32, 896)

    pre_to_z(2)

    def pre_on(k):
        sems.wait(pre.at[:, c, y, plus(zh, -k)], pre_z + k, at_core)
        return pre_to_y(k)

    cot_slot = sems.take()
    sems.start(cot.at[other], cot_other, cot_slot, at_core)

    sum_z = sems.take(4)
    total = None
    for kz in (2, 1, 3, 0):
        for k in (1, 3, 2):
            sems.wait(part_recv.at[k - 1, kz], part_y + 4 * k + kz, at_core)
        total = part_own[plus(zh, kz)]
        for k in (1, 2, 3):
            total = total + part_recv[k - 1, kz].astype(F32)
        if kz:
            sum_send[kz - 1] = total.astype(BF16)
            sems.start(sum_send.at[kz - 1], sum_recv.at[kz - 1], sum_z + kz, at_zh(kz))
    part_own[0] = total

    def pre_to_core(k):
        block = pre.at[:, c, plus(y, -k)]
        sems.start(block, block, pre_c + k, at_core)

    moving = pre_on(1)

    wait_load(ld_x)
    for k in (1, 3, 2):
        sems.wait(xs.at[:, plus(zl, -k), x], x_zl + k, at_core)
    for k in (2, 1, 3):
        sems.start(xs.at[:, :, x], xs.at[:, :, x], x_x + k, at_x(k))

    sems.settle(moving)
    moving = pre_on(3)

    def factors(k):
        group = plus(y, -k)
        sems.wait(pre.at[:, other, group], pre_c + k, at_core)

        def block(n, carry):
            h, b = n // 4, n % 4
            g = pre[0, h, group, b].astype(F32)
            u = pre[1, h, group, b].astype(F32)
            s = 1.0 / (1.0 + jnp.exp(-g))
            gs = g * s
            act[h, b] = (gs * u).astype(BF16)
            f_up[h, group, b] = gs
            f_gate[h, group, b] = u * s * (1.0 + g * (1.0 - s))
            return carry

        lax.fori_loop(0, 8, block, 0)
        mine = cot[c, group].reshape(128, 256)
        theirs = cot_other[group].reshape(128, 256)
        for i in range(7):
            at = pl.ds(i * TILE, TILE)
            tile = dot(act[c, :, :, at].reshape(128, TILE), mine, TN)
            tile = tile + dot(act[other, :, :, at].reshape(128, TILE), theirs, TN)
            if k:
                tile = tile + dwg[at, :]
            dwg[at, :] = tile

    total = part_own[0]
    for kz in (1, 3, 2):
        sems.wait(sum_recv.at[kz - 1], sum_z + kz, at_core)
        total = total + sum_recv[kz - 1].astype(F32)

    hid[c, y, zh] = total.astype(BF16)
    hid_z = sems.take(4)
    hid_y = sems.take(16)
    hid_c0 = sems.take(4)
    hid_c = sems.take(4)
    for k in (1, 3, 2):
        block = hid.at[c, y, zh]
        sems.start(block, block, hid_z + k, at_zh(k))

    def hid_on(kz):
        block = hid.at[c, y, plus(zh, -kz)]
        for k in (1, 3, 2):
            sems.start(block, block, hid_y + 4 * k + kz, at_y(k))
        sems.start(block, block, hid_c0 + kz, at_core)

    hid_on(0)
    sems.settle(moving)
    pre_on(2)
    pre_to_core(0)
    sems.wait(cot_other, cot_slot, at_core)
    factors(0)


    def pre_arrive(k):
        group = plus(y, -k)
        for kz in (0, 1, 3, 2):
            sems.wait(pre.at[:, c, group, plus(zh, -kz)], pre_y + 4 * k + kz, at_core)
        pre_to_core(k)

    for k in (1, 3):
        sems.wait(hid.at[c, y, plus(zh, -k)], hid_z + k, at_core)
        hid_on(k)
    pre_arrive(1)
    pre_arrive(3)
    factors(1)
    sems.wait(hid.at[c, y, plus(zh, -2)], hid_z + 2, at_core)
    hid_on(2)
    factors(3)
    pre_arrive(2)

    ig_x = sems.take(16)

    def hid_arrive(k):
        group = plus(y, -k)
        for kz in (0, 1, 3, 2):
            sems.wait(hid.at[c, group, plus(zh, -kz)], hid_y + 4 * k + kz, at_core)
        sems.start(hid.at[c, group], hid.at[c, group], hid_c + k, at_core)

    def input_rows(k):
        group = plus(y, -k)
        if k:
            sems.wait(hid.at[other, group], hid_c + k, at_core)
        else:
            for kz in range(4):
                sems.wait(hid.at[other, group, plus(zh, -kz)], hid_c0 + kz, at_core)
        rows = hid[:, group].astype(F32)
        gate[k] = (rows * f_gate[:, group]).astype(BF16).reshape(256, 896)
        up[k] = (rows * f_up[:, group]).astype(BF16).reshape(256, 896)
        rows = dot(gate[k], gw[...], NT) + dot(up[k], uw[...], NT)
        rows = rows.reshape(2, 4, 32, 256)
        ig_send[k] = rows.astype(BF16)
        for j in (2, 1, 3):
            sems.start(
                ig_send.at[k, :, plus(x, j)], ig_recv.at[k, j - 1], ig_x + 4 * k + j, at_x(j)
            )
        own = rows[:, 0]
        for j in (1, 2, 3):
            own = jnp.where(x == j, rows[:, j], own)
        ig_own[k] = own

    def weight_rows(k):
        left = xs[:, plus(y, -k)].reshape(256, 256)
        for total_ref, rows_ref in ((gwg, gate), (uwg, up)):
            product = dot(left, rows_ref[k], TN)
            if k:
                product = product + total_ref[...]
            total_ref[...] = product

    def reduce_x(k):
        group = plus(y, -k)
        for j in (1, 3, 2):
            sems.wait(ig_recv.at[k, j - 1], ig_x + 4 * k + j, at_core)
        value = ig_own[k]
        for j in (0, 1, 2):
            value = value + ig_recv[k, j].astype(F32)

        @pl.when(group == zl)
        def _():
            ig_mine[...] = value

        @pl.when(group != zl)
        def _():
            zl_send[k] = value
            to_zl(k).start()

    def to_zl(k):
        group = plus(y, -k)
        return pltpu.make_async_remote_copy(
            src_ref=zl_send.at[k],
            dst_ref=zl_recv.at[zl],
            send_sem=zl_ss.at[k],
            recv_sem=zl_rs.at[zl],
            device_id={"dep": group * 4 + x},
            device_id_type=MESH,
        )

    input_rows(0)
    for k in (1, 3, 2):
        sems.wait(xs.at[:, :, plus(x, -k)], x_x + k, at_core)
    weight_rows(0)
    factors(2)
    keep_tiles(dwg, lambda i, j: dm[j, i], (7, 2))
    stores = [load(dwg, dwg_out)]
    reduce_x(0)
    hid_arrive(1)
    hid_arrive(3)
    input_rows(1)
    input_rows(3)
    hid_arrive(2)
    weight_rows(1)
    input_rows(2)
    reduce_x(1)
    reduce_x(3)
    weight_rows(3)
    weight_rows(2)
    keep_tiles(gwg, lambda i, j: gm[i, j])
    stores.append(load(gwg, gwg_out))
    keep_tiles(uwg, lambda i, j: um[i, j])
    stores.append(load(uwg, uwg_out))
    reduce_x(2)

    value = ig_mine[...]
    for k in (1, 2, 3):
        source = plus(zl, k)
        pltpu.make_async_remote_copy(
            src_ref=zl_recv.at[source],
            dst_ref=zl_recv.at[source],
            send_sem=zl_ss.at[0],
            recv_sem=zl_rs.at[source],
            device_id=at_core,
            device_id_type=MESH,
        ).wait_recv()
        value = value + zl_recv[source]
    ig_res[...] = value.astype(BF16)
    stores.append(load(ig_res, ig_out))
    sems.drain()
    for k in range(4):

        @pl.when(plus(y, -k) != zl)
        def _():
            to_zl(k).wait_send()

    for copy in stores:
        copy.wait()


def store(*refs):
    copies = [
        pltpu.make_async_copy(src, dst, refs[8].at[n])
        for n, (src, dst) in enumerate(zip(refs[:4], refs[4:8]))
    ]
    for copy in copies:
        copy.start()
    for copy in copies:
        copy.wait()


SENDS = 128
RECVS = 128


def on_device(x_saved, gate_pre, up_pre, out_grad, gate_weight, up_weight, down_weight, gate_mask, up_mask, down_mask):
    any_ = pl.BlockSpec(memory_space=pl.ANY)
    hbm = pl.BlockSpec(memory_space=pltpu.HBM)
    vmem = lambda *shape: pltpu.VMEM(shape, BF16)
    vmem32 = lambda *shape: pltpu.VMEM(shape, F32)
    outs = pl.pallas_call(
        kernel,
        name="backward",
        out_shape=(
            jax.ShapeDtypeStruct((2, 32, 256), BF16),
            jax.ShapeDtypeStruct((256, 896), F32),
            jax.ShapeDtypeStruct((256, 896), F32),
            jax.ShapeDtypeStruct((896, 256), F32),
        ),
        in_specs=[hbm] * 10,
        out_specs=(any_,) * 4,
        scratch_shapes=[
            vmem(2, 4, 4, 32, 256),
            vmem(4, 4, 32, 256),
            vmem(2, 4, 4, 32, 256),
            vmem(2, 2, 4, 4, 32, 896),
            vmem(2, 4, 4, 32, 896),
            vmem32(2, 4, 4, 32, 896),
            vmem32(2, 4, 4, 32, 896),
            vmem(2, 4, 32, 896),
            vmem(4, 256, 896),
            vmem(4, 256, 896),
            vmem(256, 896),
            vmem(256, 896),
            vmem(2, 896, 256),
            vmem32(4, 32, 896),
            vmem(3, 4, 32, 896),
            vmem(3, 4, 32, 896),
            vmem(3, 32, 896),
            vmem(3, 32, 896),
            vmem32(4, 2, 32, 256),
            vmem(4, 2, 4, 32, 256),
            vmem(4, 3, 2, 32, 256),
            vmem32(2, 32, 256),
            vmem32(4, 2, 32, 256),
            vmem32(4, 2, 32, 256),
            vmem(2, 32, 256),
            vmem32(256, 896),
            vmem32(256, 896),
            vmem32(896, 256),
            pltpu.SMEM((2, 7), jnp.int32),
            pltpu.SMEM((2, 7), jnp.int32),
            pltpu.SMEM((2, 7), jnp.int32),
            pltpu.SemaphoreType.DMA((16,)),
            pltpu.SemaphoreType.DMA((SENDS,)),
            pltpu.SemaphoreType.DMA((RECVS,)),
            pltpu.SemaphoreType.DMA((4,)),
            pltpu.SemaphoreType.DMA((4,)),
        ],
        compiler_params=pltpu.CompilerParams(
            collective_id=0, has_side_effects=True, vmem_limit_bytes=48 << 20
        ),
    )(
        *(
            pltpu.with_memory_space_constraint(value, pltpu.HBM)
            for value in (
                x_saved.reshape(2, 32, 256), gate_pre, up_pre, out_grad.reshape(2, 32, 256),
                gate_weight, up_weight, down_weight, gate_mask, up_mask, down_mask.T,
            )
        ),
    )
    outs = pl.pallas_call(
        store,
        name="store",
        out_shape=[jax.ShapeDtypeStruct(value.shape, value.dtype) for value in outs],
        in_specs=[any_] * 4,
        out_specs=[hbm] * 4,
        scratch_shapes=[pltpu.SemaphoreType.DMA((4,))],
        compiler_params=pltpu.CompilerParams(vmem_limit_bytes=1 << 20),
    )(*(pltpu.with_memory_space_constraint(value, pltpu.VMEM) for value in outs))
    return (outs[0].reshape(64, 256), *outs[1:])


def solution(mesh):
    return jax.shard_map(
        on_device,
        mesh=mesh,
        in_specs=(
            P("dep", ("inp", "out")),
            P(("inp", "out"), "dep"),
            P(("inp", "out"), "dep"),
            P("dep", ("inp", "out")),
            P(("inp", "out"), "dep"),
            P(("inp", "out"), "dep"),
            P("dep", ("inp", "out")),
            P(("inp", "out"), "dep"),
            P(("inp", "out"), "dep"),
            P("dep", ("inp", "out")),
        ),
        out_specs=(
            P("dep", ("inp", "out")),
            P(("inp", "out"), "dep"),
            P(("inp", "out"), "dep"),
            P("dep", ("inp", "out")),
        ),
        check_vma=False,
    )
```

```python
import functools

import jax
import jax.numpy as jnp
from jax import lax
from jax.experimental import pallas as pl
from jax.experimental.pallas import tpu as pltpu
from jax.sharding import PartitionSpec as P

TILE = 128
MESH = pl.DeviceIdType.MESH
PARTS = ((0, 512), (512, 384))
F32 = jnp.float32
BF16 = jnp.bfloat16
NT = (((1,), (1,)), ((), ()))
TN = (((0,), (0,)), ((), ()))


def dot(left, right, dims):
    return lax.dot_general(left, right, dims, preferred_element_type=F32)


class Sems:
    def __init__(self, send, recv):
        self.send, self.recv = send, recv
        self.sends = self.recvs = 0
        self.started = []

    def take(self, count=1):
        first = self.recvs
        self.recvs += count
        return first

    def start(self, src, dst, slot, device):
        copy = pltpu.make_async_remote_copy(
            src_ref=src,
            dst_ref=dst,
            send_sem=self.send.at[self.sends],
            recv_sem=self.recv.at[slot],
            device_id=device,
            device_id_type=MESH,
        )
        self.sends += 1
        copy.start()
        self.started.append(copy)
        return copy

    def wait(self, dst, slot, device):
        pltpu.make_async_remote_copy(
            src_ref=dst,
            dst_ref=dst,
            send_sem=self.send.at[0],
            recv_sem=self.recv.at[slot],
            device_id=device,
            device_id_type=MESH,
        ).wait_recv()

    def drain(self):
        for copy in self.started:
            copy.wait_send()


def keep_tiles(ref, mask, tiles=(2, 7), where=()):
    rows, cols = tiles
    for i in range(rows):
        for j in range(cols):
            at = (*where, pl.ds(i * TILE, TILE), pl.ds(j * TILE, TILE))
            ref[at] = (ref[at].astype(F32) * mask(i, j).astype(F32)).astype(ref.dtype)


def kernel(
    x_in, g_in, u_in, og_in, gw_in, uw_in, dw_in, gm_in, um_in, dm_in,
    ig_out, gwg, uwg, dwg,
    cot, cot_other, xs, pre, hid, f_gate, f_up, act, gate, up, gw, uw, dw,
    part_own, part_send, part_recv, sum_mine, sum_send, sum_recv,
    ig_all, ig_own, ig_send, ig_recv, ig_mine, zl_send, zl_recv,
    gm, um, dm, local, send, recv, zh_ss, zh_rs, zl_ss, zl_rs,
):
    y = lax.axis_index("inp")
    out = lax.axis_index("out")
    dep = lax.axis_index("dep")
    zh, c = out // 2, out % 2
    zl, x = dep // 4, dep % 4
    other = 1 - c
    plus = lambda v, k: (v + k) % 4
    at_core = {"out": zh * 2 + other}
    at_y = lambda k: {"inp": plus(y, k)}
    at_zh = lambda k: {"out": plus(zh, k) * 2 + c}
    at_x = lambda k: {"dep": zl * 4 + plus(x, k)}
    at_zl = lambda k, core: {"out": zh * 2 + core, "dep": plus(zl, k) * 4 + x}

    loads = []

    def load(src, dst):
        copy = pltpu.make_async_copy(src, dst, local.at[len(loads)])
        copy.start()
        loads.append(copy)
        return copy


    def wait_load(copy):
        copy.wait()

    ld_og = load(og_in.at[pl.ds(c, 1)], cot.at[c, zl, pl.ds(x, 1)])
    ld_g = load(g_in, pre.at[0, c, y, zh])
    ld_u = load(u_in, pre.at[1, c, y, zh])
    ld_dw = load(dw_in, dw.at[c])
    ld_masks = [load(dm_in, dm), load(gm_in, gm), load(um_in, um)]
    ld_x = load(x_in, xs.at[:, zl, x])
    ld_gw = load(gw_in, gw)
    ld_uw = load(uw_in, uw)

    peers = [at_core]
    for k in (1, 2, 3):
        peers += [at_y(k), at_zh(k), at_x(k), at_zl(k, 0), at_zl(k, 1)]
    barrier = pltpu.get_barrier_semaphore()
    for device in peers:
        pl.semaphore_signal(barrier, inc=1, device_id=device, device_id_type=MESH)
    pl.semaphore_wait(barrier, len(peers))

    sems = Sems(send, recv)

    og_slot = sems.take(8)
    sems.start(og_in.at[other], cot.at[c, zl, x], og_slot + c, at_core)
    for k in (2, 1, 3):
        for h in (0, 1):
            sems.start(og_in.at[h], cot.at[c, zl, x], og_slot + 2 * k + c, at_zl(k, h))

    pre_z = sems.take(4)
    pre_y = sems.take(16)
    pre_c = sems.take(4)

    def pre_to_y(kz):
        block = pre.at[:, c, y, plus(zh, -kz)]
        for k in (1, 3):
            sems.start(block, block, pre_y + 4 * k + kz, at_y(k))

    wait_load(ld_g)
    wait_load(ld_u)
    pre_to_y(0)

    def pre_to_z(k):
        block = pre.at[:, c, y, zh]
        sems.start(block, block, pre_z + k, at_zh(k))

    pre_to_z(1)
    pre_to_z(3)


    wait_load(ld_dw)
    for copy in ld_masks:
        wait_load(copy)
    keep_tiles(dw, lambda i, j: dm[j, i], (7, 2), (c,))
    dw_slot = sems.take()
    sems.start(dw.at[c], dw.at[c], dw_slot, at_core)

    og_x = sems.take(16)

    def cot_to_x(kz):
        block = cot.at[:, plus(zl, -kz), x]
        for k in (1, 3, 2):
            sems.start(block, block, og_x + 4 * k + kz, at_x(k))

    wait_load(ld_og)
    sems.wait(cot.at[other, zl, x], og_slot + other, at_core)
    cot_to_x(0)
    for k in (1, 3, 2):
        for f in (0, 1):
            sems.wait(cot.at[f, plus(zl, -k), x], og_slot + 2 * k + f, at_core)
        cot_to_x(k)

    x_zl = sems.take(4)
    x_x = sems.take(4)
    for k in (2, 1, 3):
        sems.start(x_in, xs.at[:, zl, x], x_zl + k, at_zl(k, c))

    sems.wait(dw.at[other], dw_slot, at_core)

    units = [pl.ds(*part) for part in PARTS]
    part_y = sems.take(32)

    def partial(n, p):
        column = plus(x, n)
        if n and not p:
            for kz in (0, 1, 3, 2):
                sems.wait(
                    cot.at[:, plus(zl, -kz), column], og_x + 4 * (4 - n) + kz, at_core
                )
        at = units[p]
        rows = [cot[f, :, column].reshape(128, 256) for f in (0, 1)]
        part = dot(rows[0], dw[0, at], NT) + dot(rows[1], dw[1, at], NT)
        part = part.reshape(4, 32, PARTS[p][1])
        part_own[n, :, :, at] = part
        part_send[n, :, :, at] = part.astype(BF16)
        for k in (2, 1, 3):
            sems.start(
                part_send.at[n, plus(y, k), :, at],
                part_recv.at[n, k - 1, :, at],
                part_y + 16 * p + 4 * n + k,
                at_y(k),
            )

    for p in (0, 1):
        for n in (0, 1, 3, 2):
            partial(n, p)

    wait_load(ld_gw)
    keep_tiles(gw, lambda i, j: gm[i, j])
    wait_load(ld_uw)
    keep_tiles(uw, lambda i, j: um[i, j])

    cot_slot = sems.take()
    sems.start(cot.at[other], cot_other, cot_slot, at_core)

    def pre_opposite():
        for k in (1, 3):
            block = plus(zh, -k)
            sems.wait(pre.at[:, c, y, block], pre_z + k, at_core)
            block = pre.at[k // 2, c, y, block]
            sems.start(block, block, pre_z + 2 - 2 * (k // 2), at_zh(k))

    pre_opposite()

    def to_zh(n, p):
        return pltpu.make_async_remote_copy(
            src_ref=sum_send.at[n, :, units[p]],
            dst_ref=sum_recv.at[zh, :, units[p]],
            send_sem=zh_ss.at[p, n],
            recv_sem=zh_rs.at[p, zh],
            device_id={"out": plus(x, n) * 2 + c},
            device_id_type=MESH,
        )

    def sum_y(n, p):
        at = units[p]
        for k in (1, 3, 2):
            sems.wait(part_recv.at[n, k - 1, :, at], part_y + 16 * p + 4 * n + k, at_core)
        total = part_own[n, y, :, at]
        for k in (0, 1, 2):
            total = total + part_recv[n, k, :, at].astype(F32)

        @pl.when(plus(x, n) == zh)
        def _():
            sum_mine[:, at] = total

        @pl.when(plus(x, n) != zh)
        def _():
            sum_send[n, :, at] = total.astype(BF16)
            to_zh(n, p).start()

    for n in (0, 1, 3, 2):
        sum_y(n, 0)
    for n in (0, 1, 3, 2):
        sum_y(n, 1)

    def zh_wait(p):
        for k in (1, 3, 2):
            source = plus(zh, k)
            pltpu.make_async_remote_copy(
                src_ref=sum_recv.at[source, :, units[p]],
                dst_ref=sum_recv.at[source, :, units[p]],
                send_sem=zh_ss.at[0, 0],
                recv_sem=zh_rs.at[p, source],
                device_id=at_core,
                device_id_type=MESH,
            ).wait_recv()

    def zh_drain():
        for p in (0, 1):
            for n in range(4):

                @pl.when(plus(x, n) != zh)
                def _():
                    to_zh(n, p).wait_send()


    def pre_to_core(k):
        block = pre.at[:, c, plus(y, -k)]
        sems.start(block, block, pre_c + k, at_core)

    pre_to_y(1)
    pre_to_y(3)

    def factors(k):
        group = plus(y, -k)
        sems.wait(pre.at[:, other, group], pre_c + k, at_core)

        def block(n, carry):
            h, b = n // 4, n % 4
            g = pre[0, h, group, b].astype(F32)
            u = pre[1, h, group, b].astype(F32)
            s = 1.0 / (1.0 + jnp.exp(-g))
            gs = g * s
            act[h, b] = (gs * u).astype(BF16)
            f_up[h, group, b] = gs
            f_gate[h, group, b] = u * s * (1.0 + g * (1.0 - s))
            return carry

        lax.fori_loop(0, 8, block, 0)
        mine = cot[c, group].reshape(128, 256)
        theirs = cot_other[group].reshape(128, 256)
        for i in range(7):
            at = pl.ds(i * TILE, TILE)
            tile = dot(act[c, :, :, at].reshape(128, TILE), mine, TN)
            tile = tile + dot(act[other, :, :, at].reshape(128, TILE), theirs, TN)
            if k:
                tile = tile + dwg[at, :]
            dwg[at, :] = tile

    hid_z = sems.take(8)
    hid_y = sems.take(32)
    hid_c0 = sems.take(8)
    hid_c = sems.take(8)

    def hid_on(kz, p):
        block = hid.at[c, y, plus(zh, -kz), :, units[p]]
        for k in (1, 3, 2):
            sems.start(block, block, hid_y + 16 * p + 4 * k + kz, at_y(k))
        sems.start(block, block, hid_c0 + 4 * p + kz, at_core)

    def hid_begin(p):
        at = units[p]
        zh_wait(p)
        total = sum_mine[:, at]
        for k in (1, 2, 3):
            total = total + sum_recv[plus(zh, k), :, at].astype(F32)
        hid[c, y, zh, :, at] = total.astype(BF16)
        block = hid.at[c, y, zh, :, at]
        for k in (1, 3, 2):
            sems.start(block, block, hid_z + 4 * p + k, at_zh(k))
        hid_on(0, p)

    def hid_next(k, p):
        sems.wait(hid.at[c, y, plus(zh, -k), :, units[p]], hid_z + 4 * p + k, at_core)
        hid_on(k, p)

    hid_begin(0)
    for n in (0, 1):
        sems.wait(pre.at[n, c, y, plus(zh, -2)], pre_z + 2 - 2 * n, at_core)
    pre_to_y(2)
    hid_begin(1)
    pre_to_core(0)

    wait_load(ld_x)
    for k in (1, 3, 2):
        sems.wait(xs.at[:, plus(zl, -k), x], x_zl + k, at_core)
    for k in (2, 1, 3):
        sems.start(xs.at[:, :, x], xs.at[:, :, x], x_x + k, at_x(k))


    def pre_arrive(k):
        group = plus(y, -k)
        if k == 2:
            for n in (0, 1):
                sems.wait(pre.at[n, c, group], pre_y + 8 + n, at_core)
        else:
            for kz in (0, 1, 3, 2):
                sems.wait(pre.at[:, c, group, plus(zh, -kz)], pre_y + 4 * k + kz, at_core)
            n = k // 2
            block = pre.at[n, c, group]
            sems.start(block, block, pre_y + 8 + n, at_y(k))
        pre_to_core(k)


    ig_x = sems.take(16)

    def hid_arrive(k, p):
        group, at = plus(y, -k), units[p]
        for kz in (0, 1, 3, 2):
            sems.wait(
                hid.at[c, group, plus(zh, -kz), :, at], hid_y + 16 * p + 4 * k + kz, at_core
            )
        block = hid.at[c, group, :, :, at]
        sems.start(block, block, hid_c + 4 * p + k, at_core)

    def input_rows(k, p):
        group, at = plus(y, -k), units[p]
        if k:
            sems.wait(hid.at[other, group, :, :, at], hid_c + 4 * p + k, at_core)
        else:
            for kz in range(4):
                sems.wait(
                    hid.at[other, group, plus(zh, -kz), :, at], hid_c0 + 4 * p + kz, at_core
                )
        rows = hid[:, group, :, :, at].astype(F32)
        gate[k, :, at] = (rows * f_gate[:, group, :, :, at]).astype(BF16).reshape(256, -1)
        up[k, :, at] = (rows * f_up[:, group, :, :, at]).astype(BF16).reshape(256, -1)
        rows = dot(gate[k, :, at], gw[:, at], NT) + dot(up[k, :, at], uw[:, at], NT)
        rows = rows.reshape(2, 4, 32, 256)
        if not p:
            ig_all[k] = rows
            return
        rows = rows + ig_all[k]
        ig_send[k] = rows.astype(BF16)
        for j in (2, 1, 3):
            sems.start(
                ig_send.at[k, :, plus(x, j)], ig_recv.at[k, j - 1], ig_x + 4 * k + j, at_x(j)
            )
        own = rows[:, 0]
        for j in (1, 2, 3):
            own = jnp.where(x == j, rows[:, j], own)
        ig_own[k] = own

    def weight_rows(k, p):
        at = units[p]
        left = xs[:, plus(y, -k)].reshape(256, 256)
        for total_ref, rows_ref in ((gwg, gate), (uwg, up)):
            product = dot(left, rows_ref[k, :, at], TN)
            if k:
                product = product + total_ref[:, at]
            total_ref[:, at] = product

    def reduce_x(k):
        group = plus(y, -k)
        for j in (1, 3, 2):
            sems.wait(ig_recv.at[k, j - 1], ig_x + 4 * k + j, at_core)
        value = ig_own[k]
        for j in (0, 1, 2):
            value = value + ig_recv[k, j].astype(F32)

        @pl.when(group == zl)
        def _():
            ig_mine[...] = value

        @pl.when(group != zl)
        def _():
            zl_send[k] = value
            to_zl(k).start()

    def to_zl(k):
        group = plus(y, -k)
        return pltpu.make_async_remote_copy(
            src_ref=zl_send.at[k],
            dst_ref=zl_recv.at[zl],
            send_sem=zl_ss.at[k],
            recv_sem=zl_rs.at[zl],
            device_id={"dep": group * 4 + x},
            device_id_type=MESH,
        )

    sems.wait(cot_other, cot_slot, at_core)
    factors(0)
    for k in (1, 3, 2):
        hid_next(k, 0)
    pre_arrive(1)
    pre_arrive(3)
    input_rows(0, 0)
    factors(1)
    hid_next(1, 1)
    hid_next(3, 1)
    for k in (1, 3, 2):
        sems.wait(xs.at[:, :, plus(x, -k)], x_x + k, at_core)
    weight_rows(0, 0)
    hid_next(2, 1)
    factors(3)
    input_rows(0, 1)
    hid_arrive(1, 0)
    hid_arrive(3, 0)
    weight_rows(0, 1)
    input_rows(1, 0)
    input_rows(3, 0)
    pre_arrive(2)
    hid_arrive(2, 0)
    weight_rows(1, 0)
    factors(2)
    weight_rows(3, 0)
    input_rows(2, 0)
    reduce_x(0)
    weight_rows(2, 0)
    hid_arrive(1, 1)
    hid_arrive(3, 1)
    hid_arrive(2, 1)
    input_rows(1, 1)
    input_rows(3, 1)
    input_rows(2, 1)
    weight_rows(1, 1)
    reduce_x(1)
    weight_rows(3, 1)
    reduce_x(3)
    weight_rows(2, 1)
    reduce_x(2)
    keep_tiles(dwg, lambda i, j: dm[j, i], (7, 2))
    keep_tiles(gwg, lambda i, j: gm[i, j])
    keep_tiles(uwg, lambda i, j: um[i, j])

    value = ig_mine[...]
    for k in (1, 2, 3):
        source = plus(zl, k)
        pltpu.make_async_remote_copy(
            src_ref=zl_recv.at[source],
            dst_ref=zl_recv.at[source],
            send_sem=zl_ss.at[0],
            recv_sem=zl_rs.at[source],
            device_id=at_core,
            device_id_type=MESH,
        ).wait_recv()
        value = value + zl_recv[source]
    ig_out[...] = value.astype(BF16)
    sems.drain()
    zh_drain()
    for k in range(4):

        @pl.when(plus(y, -k) != zl)
        def _():
            to_zl(k).wait_send()


def store(*refs):
    copies = [
        pltpu.make_async_copy(src, dst, refs[8].at[n])
        for n, (src, dst) in enumerate(zip(refs[:4], refs[4:8]))
    ]
    for copy in copies:
        copy.start()
    for copy in copies:
        copy.wait()


SENDS = 160
RECVS = 192


def on_device(x_saved, gate_pre, up_pre, out_grad, gate_weight, up_weight, down_weight, gate_mask, up_mask, down_mask):
    any_ = pl.BlockSpec(memory_space=pl.ANY)
    hbm = pl.BlockSpec(memory_space=pltpu.HBM)
    vmem = lambda *shape: pltpu.VMEM(shape, BF16)
    vmem32 = lambda *shape: pltpu.VMEM(shape, F32)
    outs = pl.pallas_call(
        kernel,
        name="backward",
        out_shape=(
            vmem(2, 32, 256),
            vmem32(256, 896),
            vmem32(256, 896),
            vmem32(896, 256),
        ),
        in_specs=[hbm] * 10,
        out_specs=(pl.BlockSpec(memory_space=pltpu.VMEM),) * 4,
        scratch_shapes=[
            vmem(2, 4, 4, 32, 256),
            vmem(4, 4, 32, 256),
            vmem(2, 4, 4, 32, 256),
            vmem(2, 2, 4, 4, 32, 896),
            vmem(2, 4, 4, 32, 896),
            vmem32(2, 4, 4, 32, 896),
            vmem32(2, 4, 4, 32, 896),
            vmem(2, 4, 32, 896),
            vmem(4, 256, 896),
            vmem(4, 256, 896),
            vmem(256, 896),
            vmem(256, 896),
            vmem(2, 896, 256),
            vmem32(4, 4, 32, 896),
            vmem(4, 4, 32, 896),
            vmem(4, 3, 32, 896),
            vmem32(32, 896),
            vmem(4, 32, 896),
            vmem(4, 32, 896),
            vmem32(4, 2, 4, 32, 256),
            vmem32(4, 2, 32, 256),
            vmem(4, 2, 4, 32, 256),
            vmem(4, 3, 2, 32, 256),
            vmem32(2, 32, 256),
            vmem32(4, 2, 32, 256),
            vmem32(4, 2, 32, 256),
            pltpu.SMEM((2, 7), jnp.int32),
            pltpu.SMEM((2, 7), jnp.int32),
            pltpu.SMEM((2, 7), jnp.int32),
            pltpu.SemaphoreType.DMA((16,)),
            pltpu.SemaphoreType.DMA((SENDS,)),
            pltpu.SemaphoreType.DMA((RECVS,)),
            pltpu.SemaphoreType.DMA((2, 4)),
            pltpu.SemaphoreType.DMA((2, 4)),
            pltpu.SemaphoreType.DMA((4,)),
            pltpu.SemaphoreType.DMA((4,)),
        ],
        compiler_params=pltpu.CompilerParams(
            collective_id=0, has_side_effects=True, vmem_limit_bytes=48 << 20
        ),
    )(
        *(
            pltpu.with_memory_space_constraint(value, pltpu.HBM)
            for value in (
                x_saved.reshape(2, 32, 256), gate_pre, up_pre, out_grad.reshape(2, 32, 256),
                gate_weight, up_weight, down_weight, gate_mask, up_mask, down_mask.T,
            )
        ),
    )
    outs = pl.pallas_call(
        store,
        name="store",
        out_shape=[jax.ShapeDtypeStruct(value.shape, value.dtype) for value in outs],
        in_specs=[any_] * 4,
        out_specs=[hbm] * 4,
        scratch_shapes=[pltpu.SemaphoreType.DMA((4,))],
        compiler_params=pltpu.CompilerParams(vmem_limit_bytes=1 << 20),
    )(*(pltpu.with_memory_space_constraint(value, pltpu.VMEM) for value in outs))
    return (outs[0].reshape(64, 256), *outs[1:])


def solution(mesh):
    return jax.shard_map(
        on_device,
        mesh=mesh,
        in_specs=(
            P("dep", ("inp", "out")),
            P(("inp", "out"), "dep"),
            P(("inp", "out"), "dep"),
            P("dep", ("inp", "out")),
            P(("inp", "out"), "dep"),
            P(("inp", "out"), "dep"),
            P("dep", ("inp", "out")),
            P(("inp", "out"), "dep"),
            P(("inp", "out"), "dep"),
            P("dep", ("inp", "out")),
        ),
        out_specs=(
            P("dep", ("inp", "out")),
            P(("inp", "out"), "dep"),
            P(("inp", "out"), "dep"),
            P("dep", ("inp", "out")),
        ),
        check_vma=False,
    )
```
